32 devices in a mesh: groups: 2 (over y), row: 8 (over z, x), col: 2 (over core).
Axes of the slice: x: 2, y: 2, z: 4, core: 2. Of those that a mesh axis runs over, the one named last changes fastest.
Arguments:
- object_slices: float32 [4, 2, 2048, 512], P(None, None, ('groups', 'row'), 'col'), parts along dimension 2, may hold values from -4 to 4
- probe: float32 [16, 2, 128, 128], P('groups'), parts along dimension 0, may hold values from -3 to 3
- taps: float32 [2, 63], replicated, may hold values from -0.5 to 0.5
- measured: float32 [64, 128, 128], P(('groups', 'row', 'col')), parts along dimension 0, may hold values from 0.5 to 16
- positions: int32 [64, 2], P(('groups', 'row', 'col')), parts along dimension 0, may hold values from -64 to 959, as said below
Outputs:
- object_grad: float32 [4, 2, 2048, 512], P(None, None, ('groups', 'row'), 'col'), parts along dimension 2
- new_probe: float32 [16, 2, 16384], P('groups', None, ('row', 'col')), parts along dimension 0
The draws below stay inside these ranges and needn't reach their ends.
There are 2 independent parts, one for each index of `groups`. The reference program is written for one: setup_inputs(seed, part) draws one part's arguments, and reference() takes and returns one part's arrays. A program takes and returns all parts, laid end to end along the dimension named above; an argument that names none is the same for every part. Nothing has to cross between parts.
Inputs may be any that keep to these rules, and one draw needn't show every extreme that they name: `positions`: record r belongs to device d = r // 2 in row-major order over the (row, col) device grid, with tile indices (i, q); its row lies in [i * 128 - 128/2, (i + 1) * 128 - 128/2) and its column in [q * 256 - 128/2, (q + 1) * 256 - 128/2).
All inputs are finite; a program needn't handle non-finite values.
Results may differ from the reference program's by a relative error of at most 0.0003.
Values sent between devices are 32-bit elements; how exact they have to be, the bound alone decides.
A program may use at most 64 MiB of HBM per device.

```python
import math
import jax
import jax.numpy as jnp
from jax import lax

SLICES = 4
MODES = 8
WINDOW = 128
TAPS = 63
TILE_R = 128
TILE_C = 256
REC_DEV = 2
OBJ_R = 1024
OBJ_C = 512
RECORDS = 32


def draw_positions(key, part):
    tiles_across = OBJ_C // TILE_C
    record_idx = jnp.arange(RECORDS, dtype=jnp.int32)
    device_idx = record_idx // REC_DEV
    tile_row = device_idx // tiles_across
    tile_col = device_idx % tiles_across
    key_rows, key_cols = jax.random.split(jax.random.fold_in(key, 11))
    row_off = jax.random.randint(key_rows, (RECORDS,), 0, TILE_R, dtype=jnp.int32)
    col_off = jax.random.randint(key_cols, (RECORDS,), 0, TILE_C, dtype=jnp.int32)
    row_off = row_off.at[0].set(0)
    row_off = row_off.at[RECORDS - 1].set(TILE_R - 1)
    col_off = col_off.at[RECORDS - 1].set(TILE_C - 1)
    rows = row_off + tile_row * TILE_R - WINDOW // 2
    cols = col_off + tile_col * TILE_C - WINDOW // 2
    return jnp.stack([rows, cols], axis=1)


def shard_levels(key, dims, shards, smallest, high):
    level, own = 1.0, jax.random.fold_in(key, 6)
    for dim, parts in shards:
        draws = jnp.exp(jax.random.uniform(jax.random.fold_in(own, dim), (parts,), jnp.float32, smallest / len(shards), high / len(shards)))
        level = level * jnp.repeat(draws, dims[dim] // parts).reshape([-1 if axis == dim else 1 for axis in range(len(dims))])
    return level


def bell_draw(stream_key, shape, scale, bound, cuts=(), held_as=jnp.bfloat16):
    level = shard_levels(stream_key, shape, cuts, -0.22, 0.18) if cuts else 1.0
    array = jax.random.normal(stream_key, shape, jnp.float32) * scale * level
    return jnp.minimum(jnp.maximum(array, -bound), bound).astype(held_as)


def setup_inputs(seed: int = 0, part: int = 0) -> dict:
    seeds = jax.random.split(jax.random.key(seed), 6)
    part_splits = jax.random.split(jax.random.fold_in(seeds[5], part), 6)
    return {
        "object_slices": bell_draw(part_splits[0], (SLICES, 2, OBJ_R, OBJ_C), 0.7071, 4.0, ((2, 8), (3, 2)), jnp.float32),
        "probe": bell_draw(part_splits[1], (MODES, 2, WINDOW, WINDOW), 0.5, 3.0, (), jnp.float32),
        "taps": bell_draw(seeds[2], (2, TAPS), 0.09, 0.5, (), jnp.float32),
        "measured": jnp.clip(jnp.exp(math.log(16.0) - 3.465736 * jax.random.uniform(part_splits[3], (RECORDS, WINDOW, WINDOW), jnp.float32) ** shard_levels(part_splits[3], (RECORDS, WINDOW, WINDOW), ((0, 16),), -0.2, 0.2)), 0.5, 16.0),
        "positions": draw_positions(jax.random.fold_in(jax.random.fold_in(seeds[5], part), 71), part),
    }


highest_mode = lax.Precision.HIGHEST

def einsum_exact(form, first, second):
    return jnp.einsum(form, first, second, precision=highest_mode)

def make_tables(taps, width):
    reach = taps.shape[1] // 2
    pixel_idx = lax.iota(jnp.int32, width)
    offset = pixel_idx[None, :] - pixel_idx[:, None] + reach
    tap_idx = lax.iota(jnp.int32, taps.shape[1])
    one_hot = (offset[:, :, None] == tap_idx[None, None, :]).astype(jnp.float32)
    band_re = einsum_exact('abt,t->ab', one_hot, taps[0])
    band_im = einsum_exact('abt,t->ab', one_hot, taps[1])
    phase_idx = pixel_idx[:, None] * pixel_idx[None, :] % width
    angle = 2.0 * math.pi / width * phase_idx.astype(jnp.float32)
    norm_factor = 1.0 / math.sqrt(width)
    return (band_re, band_im, jnp.cos(angle) * norm_factor, -jnp.sin(angle) * norm_factor)

def both_sides(mat_re, mat_im, wave_re, wave_im):
    left_re = einsum_exact('ab,kbc->kac', mat_re, wave_re) - einsum_exact('ab,kbc->kac', mat_im, wave_im)
    left_im = einsum_exact('ab,kbc->kac', mat_re, wave_im) + einsum_exact('ab,kbc->kac', mat_im, wave_re)
    out_re = einsum_exact('kac,dc->kad', left_re, mat_re) - einsum_exact('kac,dc->kad', left_im, mat_im)
    out_im = einsum_exact('kac,dc->kad', left_re, mat_im) + einsum_exact('kac,dc->kad', left_im, mat_re)
    return (out_re, out_im)

def record_loss(probe, patch, measured_one, tables):
    band_re, band_im, dft_re, dft_im = tables
    wave_re = probe[:, 0]
    wave_im = probe[:, 1]
    layers = patch.shape[0]
    for layer_idx in range(layers):
        obj_re = patch[layer_idx, 0]
        obj_im = patch[layer_idx, 1]
        wave_re, wave_im = (wave_re * obj_re - wave_im * obj_im, wave_re * obj_im + wave_im * obj_re)
        if layer_idx + 1 < layers:
            wave_re, wave_im = both_sides(band_re, band_im, wave_re, wave_im)
    far_re, far_im = both_sides(dft_re, dft_im, wave_re, wave_im)
    intensity = lax.optimization_barrier(jnp.sum(far_re * far_re + far_im * far_im, axis=0))
    weight = 1.0 / (8.0 * probe.shape[0])
    return 0.5 * weight * jnp.sum((intensity - measured_one) ** 2)

def accumulate(grid, probe, measured, places, tables, patch_width):
    sizes = (grid.shape[0], 2, patch_width, patch_width)

    def one_record(carry, item):
        grad_grid, grad_probe = carry
        place, measured_one = item
        zero_idx = jnp.zeros((), jnp.int32)
        starts = (zero_idx, zero_idx, place[0].astype(jnp.int32), place[1].astype(jnp.int32))
        patch = lax.dynamic_slice(grid, starts, sizes)
        grad_wave, grad_patch = jax.grad(record_loss, argnums=(0, 1))(probe, patch, measured_one, tables)
        current = lax.dynamic_slice(grad_grid, starts, sizes)
        grad_grid = lax.dynamic_update_slice(grad_grid, current + grad_patch, starts)
        return ((grad_grid, grad_probe + grad_wave), None)
    init = (jnp.zeros(grid.shape, jnp.float32), jnp.zeros(probe.shape, jnp.float32))
    (grad_grid, grad_probe), unused = lax.scan(one_record, init, (places, measured))
    return (grad_grid, grad_probe)

def gram_of(first, second):
    stacked = jnp.concatenate([first, second], axis=0)
    col_re = stacked[:, 0]
    col_im = stacked[:, 1]
    gram_re = einsum_exact('ax,bx->ab', col_re, col_re) + einsum_exact('ax,bx->ab', col_im, col_im)
    gram_im = einsum_exact('ax,bx->ab', col_re, col_im) - einsum_exact('ax,bx->ab', col_im, col_re)
    return (gram_re, gram_im)

def complex_cholesky(herm_re, herm_im):
    count = herm_re.shape[0]
    order_idx = lax.iota(jnp.int32, count)
    cols_re = []
    cols_im = []
    for col_idx in range(count):
        numer_re = herm_re[:, col_idx]
        numer_im = herm_im[:, col_idx]
        for prev_idx in range(col_idx):
            vec_re = cols_re[prev_idx]
            vec_im = cols_im[prev_idx]
            pivot_re = vec_re[col_idx]
            pivot_im = vec_im[col_idx]
            numer_re = numer_re - (vec_re * pivot_re + vec_im * pivot_im)
            numer_im = numer_im - (vec_im * pivot_re - vec_re * pivot_im)
        diag_val = jnp.sqrt(numer_re[col_idx])
        below = order_idx > col_idx
        at_diag = order_idx == col_idx
        cols_re.append(jnp.where(below, numer_re / diag_val, 0.0) + jnp.where(at_diag, diag_val, 0.0))
        cols_im.append(jnp.where(below, numer_im / diag_val, 0.0))
    return (jnp.stack(cols_re, axis=1), jnp.stack(cols_im, axis=1))

def lower_inverse(low_re, low_im):
    count = low_re.shape[0]
    unit = jnp.eye(count, dtype=low_re.dtype)
    rows_re = []
    rows_im = []
    for row_idx in range(count):
        acc_re = unit[row_idx]
        acc_im = jnp.zeros_like(unit[row_idx])
        for prev_idx in range(row_idx):
            coef_re = low_re[row_idx, prev_idx]
            coef_im = low_im[row_idx, prev_idx]
            acc_re = acc_re - (coef_re * rows_re[prev_idx] - coef_im * rows_im[prev_idx])
            acc_im = acc_im - (coef_re * rows_im[prev_idx] + coef_im * rows_re[prev_idx])
        rows_re.append(acc_re / low_re[row_idx, row_idx])
        rows_im.append(acc_im / low_re[row_idx, row_idx])
    return (jnp.stack(rows_re, axis=0), jnp.stack(rows_im, axis=0))

def orthonormalize(probe_cols, grad_cols, gram_re, gram_im, scale_out):
    modes = probe_cols.shape[0]
    trace_pp = jnp.trace(gram_re[:modes, :modes])
    trace_gg = jnp.trace(gram_re[modes:, modes:])
    factor = 0.5 * jnp.sqrt(trace_pp / (trace_gg + 1e-06))
    new_re = gram_re[:modes, :modes] - factor * (gram_re[:modes, modes:] + gram_re[modes:, :modes]) + factor * factor * gram_re[modes:, modes:]
    new_im = gram_im[:modes, :modes] - factor * (gram_im[:modes, modes:] + gram_im[modes:, :modes]) + factor * factor * gram_im[modes:, modes:]
    low_re, low_im = complex_cholesky(new_re, new_im)
    inv_re, inv_im = lower_inverse(low_re, low_im)
    right_re = inv_re.T
    right_im = -inv_im.T
    moved = probe_cols - factor * grad_cols
    moved_re = moved[:, 0]
    moved_im = moved[:, 1]
    out_re = einsum_exact('kx,kj->jx', moved_re, right_re) - einsum_exact('kx,kj->jx', moved_im, right_im)
    out_im = einsum_exact('kx,kj->jx', moved_re, right_im) + einsum_exact('kx,kj->jx', moved_im, right_re)
    return jnp.stack([out_re, out_im], axis=1) * scale_out

def reference(object_slices, probe, taps, measured, positions):
    width = probe.shape[-1]
    half = width // 2
    tables = make_tables(taps, width)
    grid = jnp.pad(object_slices, ((0, 0), (0, 0), (half, half), (half, half)))
    places = positions + half
    grad_grid, grad_probe = accumulate(grid, probe, measured, places, tables, width)
    object_grad = grad_grid[:, :, half:-half, half:-half]
    modes = probe.shape[0]
    probe_cols = probe.reshape(modes, 2, width * width)
    grad_cols = grad_probe.reshape(modes, 2, width * width)
    gram_re, gram_im = gram_of(probe_cols, grad_cols)
    new_probe = orthonormalize(probe_cols, grad_cols, gram_re, gram_im, float(width))
    return (object_grad, new_probe)
```

```python
import functools
import math

import jax
import jax.numpy as jnp
import numpy as np
from jax import lax
from jax.experimental import pallas as pl
from jax.experimental.pallas import tpu as pltpu
from jax.sharding import PartitionSpec as P

highest_mode = lax.Precision.HIGHEST
EDGE = 128


def split(value):
    high = value.astype(jnp.bfloat16)
    low = (value - high.astype(jnp.float32)).astype(jnp.bfloat16)
    return high, low


def block_matrix(mat_re, mat_im):
    top = jnp.concatenate([mat_re, -mat_im], axis=1)
    bottom = jnp.concatenate([mat_im, mat_re], axis=1)
    return jnp.concatenate([top, bottom], axis=0)


def store_matrices(mat_re, mat_im, trans_re, trans_im, slot, rights, lefts):
    plain = split(block_matrix(mat_re, mat_im))
    turned = split(block_matrix(trans_re, -trans_im))
    for place, (right, left) in ((slot, (turned, plain)), (slot + 2, (plain, turned))):
        rights[place] = jnp.concatenate([right[0], right[0], right[1]], axis=0)
        lefts[place] = jnp.concatenate([left[0], left[0], left[1]], axis=1)


def both_sides(waves, right, left):
    width = waves[0][0].shape[0]
    rows = jnp.concatenate([jnp.concatenate([re, im], axis=1) for re, im in waves], axis=0)
    high, low = split(rows)
    mid = jnp.dot(
        jnp.concatenate([high, low, high], axis=1), right, preferred_element_type=jnp.float32
    )
    parts = []
    for idx in range(len(waves)):
        part = mid[idx * width : (idx + 1) * width]
        parts.append(jnp.concatenate([part[:, :width], part[:, width:]], axis=0))
    cols = jnp.concatenate(parts, axis=1)
    high, low = split(cols)
    out = jnp.dot(
        left, jnp.concatenate([high, low, high], axis=0), preferred_element_type=jnp.float32
    )
    result = []
    for idx in range(len(waves)):
        part = out[:, idx * width : (idx + 1) * width]
        result.append((part[:width], part[width:]))
    return result


def wave_kernel(
    places, taps, ext, probe, measured, dft, gext, gprobe,
    rights, lefts, waves, far, patch, gpatch, level,
):
    modes, _, width, _ = probe.shape
    layers = ext.shape[0]
    records = measured.shape[0]
    count = taps.shape[1]
    reach = count // 2
    group = 4
    weight = 1.0 / (8.0 * modes)

    shape = (width, width)
    offset = lax.broadcasted_iota(jnp.int32, shape, 1) - lax.broadcasted_iota(jnp.int32, shape, 0)
    bands = [jnp.zeros(shape, jnp.float32) for _ in range(4)]
    for idx in range(count):
        ahead = offset == idx - reach
        behind = offset == reach - idx
        bands[0] = jnp.where(ahead, taps[0, idx], bands[0])
        bands[1] = jnp.where(ahead, taps[1, idx], bands[1])
        bands[2] = jnp.where(behind, taps[0, idx], bands[2])
        bands[3] = jnp.where(behind, taps[1, idx], bands[3])
    store_matrices(*bands, 0, rights, lefts)
    store_matrices(dft[0], dft[1], dft[0], dft[1], 1, rights, lefts)
    gext[...] = jnp.zeros_like(gext)
    gprobe[...] = jnp.zeros_like(gprobe)

    def one_record(rec, carry):
        row = places[rec, 0]
        col = places[rec, 1]
        block = pl.multiple_of((col // EDGE) * EDGE, EDGE)
        turn = col - block
        back = lax.rem(2 * EDGE - turn, 2 * EDGE)
        top = pl.multiple_of((row // 8) * 8, 8)
        drop = row - top
        tall = width + 8
        lift = lax.rem(tall - drop, tall)
        for layer in range(layers):
            for part in range(2):
                wide = ext[layer, part, pl.ds(top, tall), pl.ds(block, 2 * EDGE)]
                wide = pltpu.roll(wide, back, 1)[:, :width]
                patch[layer, part] = pltpu.roll(wide, lift, 0)[:width]
        gpatch[...] = jnp.zeros_like(gpatch)
        level[...] = jnp.zeros_like(level)

        def forward(step, carry):
            base = step * group
            now = [(probe[base + k, 0], probe[base + k, 1]) for k in range(group)]
            for layer in range(layers):
                obj_re, obj_im = patch[layer, 0], patch[layer, 1]
                now = [(a * obj_re - b * obj_im, a * obj_im + b * obj_re) for a, b in now]
                slot = 0 if layer + 1 < layers else 1
                now = both_sides(now, rights[slot], lefts[slot])
                for k in range(group):
                    if layer + 1 < layers:
                        waves[layer, base + k, 0] = now[k][0]
                        waves[layer, base + k, 1] = now[k][1]
                    else:
                        far[base + k, 0] = now[k][0]
                        far[base + k, 1] = now[k][1]
            total = level[...]
            for a, b in now:
                total = total + (a * a + b * b)
            level[...] = total
            return carry

        lax.fori_loop(0, modes // group, forward, 0)
        level[...] = (2.0 * weight) * (level[...] - measured[rec])

        def backward(step, carry):
            base = step * group
            scale = level[...]
            now = [(far[base + k, 0] * scale, far[base + k, 1] * scale) for k in range(group)]
            for layer in reversed(range(layers)):
                slot = 2 if layer + 1 < layers else 3
                now = both_sides(now, rights[slot], lefts[slot])
                if layer:
                    before = [
                        (waves[layer - 1, base + k, 0], waves[layer - 1, base + k, 1])
                        for k in range(group)
                    ]
                else:
                    before = [(probe[base + k, 0], probe[base + k, 1]) for k in range(group)]
                sum_re, sum_im = gpatch[layer, 0], gpatch[layer, 1]
                for (a, b), (c, d) in zip(now, before):
                    sum_re = sum_re + (a * c + b * d)
                    sum_im = sum_im + (b * c - a * d)
                gpatch[layer, 0] = sum_re
                gpatch[layer, 1] = sum_im
                obj_re, obj_im = patch[layer, 0], patch[layer, 1]
                now = [(a * obj_re + b * obj_im, b * obj_re - a * obj_im) for a, b in now]
            for k in range(group):
                gprobe[base + k, 0] += now[k][0]
                gprobe[base + k, 1] += now[k][1]
            return carry

        lax.fori_loop(0, modes // group, backward, 0)
        for layer in range(layers):
            for part in range(2):
                wide = jnp.concatenate([gpatch[layer, part], jnp.zeros((8, width), jnp.float32)], axis=0)
                wide = pltpu.roll(wide, drop, 0)
                wide = jnp.concatenate([wide, jnp.zeros((tall, width), jnp.float32)], axis=1)
                where = (layer, part, pl.ds(top, tall), pl.ds(block, 2 * EDGE))
                gext[where] = gext[where] + pltpu.roll(wide, turn, 1)
        return carry

    lax.fori_loop(0, records, one_record, 0)


def run_records(places, taps, ext, probe, measured):
    modes, _, width, _ = probe.shape
    layers = ext.shape[0]
    idx = np.arange(width)
    angle = 2.0 * math.pi / width * (idx[:, None] * idx[None, :] % width)
    dft = np.stack([np.cos(angle), -np.sin(angle)]) / math.sqrt(width)
    smem = pl.BlockSpec(memory_space=pltpu.SMEM)
    vmem = pl.BlockSpec(memory_space=pltpu.VMEM)
    f32 = jnp.float32
    return pl.pallas_call(
        wave_kernel,
        out_shape=(jax.ShapeDtypeStruct(ext.shape, f32), jax.ShapeDtypeStruct(probe.shape, f32)),
        in_specs=[smem, smem, vmem, vmem, vmem, vmem],
        out_specs=(vmem, vmem),
        scratch_shapes=[
            pltpu.VMEM((4, 6 * width, 2 * width), jnp.bfloat16),
            pltpu.VMEM((4, 2 * width, 6 * width), jnp.bfloat16),
            pltpu.VMEM((layers - 1, modes, 2, width, width), f32),
            pltpu.VMEM((modes, 2, width, width), f32),
            pltpu.VMEM((layers, 2, width, width), f32),
            pltpu.VMEM((layers, 2, width, width), f32),
            pltpu.VMEM((width, width), f32),
        ],
        compiler_params=pltpu.CompilerParams(vmem_limit_bytes=48 << 20),
        name="records",
    )(places, taps, ext, probe, measured, jnp.asarray(dft, f32))


def eliminate(gram_re, gram_im, probe_re, probe_im, grad_re, grad_im, scale_out):
    modes = probe_re.shape[0]
    idx = lax.broadcasted_iota(jnp.int32, (modes, modes), 0)
    lane = lax.broadcasted_iota(jnp.int32, (modes, modes), 1)
    diag = idx == lane
    w_pp, w_gg = gram_re[:modes, :modes], gram_re[modes:, modes:]
    trace_pp = jnp.sum(jnp.where(diag, w_pp, 0.0), keepdims=True)
    trace_gg = jnp.sum(jnp.where(diag, w_gg, 0.0), keepdims=True)
    factor = 0.5 * jnp.sqrt(trace_pp / (trace_gg + 1e-06))
    new_re = w_pp - factor * (gram_re[:modes, modes:] + gram_re[modes:, :modes]) + factor * factor * w_gg
    new_im = (
        gram_im[:modes, :modes]
        - factor * (gram_im[:modes, modes:] + gram_im[modes:, :modes])
        + factor * factor * gram_im[modes:, modes:]
    )
    data_re = probe_re - factor * grad_re
    data_im = factor * grad_im - probe_im
    below = lax.broadcasted_iota(jnp.int32, (modes, 1), 0)
    for step in range(modes):
        pivot = new_re[step : step + 1, step : step + 1]
        scale = 1.0 / jnp.sqrt(pivot)
        keep = below > step
        coef_re = jnp.where(keep, new_re[:, step : step + 1] * scale, 0.0)
        coef_im = jnp.where(keep, new_im[:, step : step + 1] * scale, 0.0)
        at = below == step

        def update(re, im):
            row_re = re[step : step + 1] * scale
            row_im = im[step : step + 1] * scale
            next_re = re - (coef_re * row_re - coef_im * row_im)
            next_im = im - (coef_re * row_im + coef_im * row_re)
            return jnp.where(at, row_re, next_re), jnp.where(at, row_im, next_im)

        data_re, data_im = update(data_re, data_im)
        new_re, new_im = update(new_re, new_im)
    return data_re * scale_out, data_im * (-scale_out)


def solve_kernel(scale_out, gram, probe, grad, out):
    out_re, out_im = eliminate(gram[0], gram[1], probe[0], probe[1], grad[0], grad[1], scale_out)
    out[0] = out_re
    out[1] = out_im


def gram_of(first, second):
    stacked = jnp.concatenate([first, second], axis=0)
    both = jnp.concatenate([stacked[:, 0], stacked[:, 1]], axis=0)
    full = jnp.einsum("ax,bx->ab", both, both, precision=highest_mode)
    count = stacked.shape[0]
    return jnp.stack(
        [full[:count, :count] + full[count:, count:], full[:count, count:] - full[count:, :count]]
    )


def with_halo(array, sides):
    for axis, dim, width in sides:
        devices, length = (lax.axis_size(axis), array.shape[dim])
        up = [(i, i + 1) for i in range(devices - 1)]
        down = [(j, i) for i, j in up]
        last = lax.slice_in_dim(array, length - width, length, axis=dim)
        first = lax.slice_in_dim(array, 0, width, axis=dim)
        before = lax.ppermute(last, axis, up)
        after = lax.ppermute(first, axis, down)
        array = jnp.concatenate([before, array, after], axis=dim)
    return array


def fold_axis(grad, axis, dim, half):
    devices, full = lax.axis_size(axis), grad.shape[dim]
    inner = full - 2 * half
    up = [(i, i + 1) for i in range(devices - 1)]
    down = [(j, i) for i, j in up]
    core = lax.slice_in_dim(grad, half, half + inner, axis=dim)
    before = lax.ppermute(lax.slice_in_dim(grad, half + inner, full, axis=dim), axis, up)
    after = lax.ppermute(lax.slice_in_dim(grad, 0, half, axis=dim), axis, down)
    return core + jnp.concatenate([before, after], axis=dim)


def per_device(object_slices, probe, taps, measured, positions):
    modes, _, width, _ = probe.shape
    half = width // 2
    tile_rows = object_slices.shape[2]
    tile_cols = object_slices.shape[3]
    ext = with_halo(object_slices, (("row", 2, half), ("col", 3, EDGE)))
    anchor = jnp.stack(
        [lax.axis_index("row") * tile_rows - half, lax.axis_index("col") * tile_cols - EDGE]
    )
    places = positions - anchor[None, :]
    grad_ext, grad_probe = run_records(places, taps, ext, probe, measured)
    pixels = width * width
    share = pixels // (lax.axis_size("row") * lax.axis_size("col"))
    start = lax.axis_index(("row", "col")) * share
    own_grad = lax.psum_scatter(
        grad_probe.reshape(modes, 2, pixels), ("row", "col"), scatter_dimension=2, tiled=True
    )
    own_probe = lax.dynamic_slice_in_dim(probe.reshape(modes, 2, pixels), start, share, 2)
    gram = lax.psum(gram_of(own_probe, own_grad), ("row", "col"))
    folded = fold_axis(fold_axis(grad_ext, "col", 3, EDGE), "row", 2, half)
    new_probe = pl.pallas_call(
        functools.partial(solve_kernel, float(width)),
        out_shape=jax.ShapeDtypeStruct((2, modes, share), jnp.float32),
        name="solve",
    )(gram, own_probe.transpose(1, 0, 2), own_grad.transpose(1, 0, 2))
    return (folded, new_probe.transpose(1, 0, 2))


def solution(mesh):
    placed = (
        P(None, None, ("groups", "row"), "col"),
        P("groups", None, None, None),
        P(),
        P(("groups", "row", "col"), None, None),
        P(("groups", "row", "col"), None),
    )
    return jax.shard_map(
        per_device,
        mesh=mesh,
        in_specs=placed,
        out_specs=(P(None, None, ("groups", "row"), "col"), P("groups", None, ("row", "col"))),
        check_vma=False,
    )
```

```python
import functools
import math

import jax
import jax.numpy as jnp
import numpy as np
from jax import lax
from jax.experimental import pallas as pl
from jax.experimental.pallas import tpu as pltpu
from jax.sharding import PartitionSpec as P

highest_mode = lax.Precision.HIGHEST
EDGE = 128


def split(value):
    high = value.astype(jnp.bfloat16)
    low = (value - high.astype(jnp.float32)).astype(jnp.bfloat16)
    return high, low


def block_matrix(mat_re, mat_im):
    top = jnp.concatenate([mat_re, -mat_im], axis=1)
    bottom = jnp.concatenate([mat_im, mat_re], axis=1)
    return jnp.concatenate([top, bottom], axis=0)


def store_matrices(mat_re, mat_im, trans_re, trans_im, slot, rights, lefts):
    plain = split(block_matrix(mat_re, mat_im))
    turned = split(block_matrix(trans_re, -trans_im))
    for place, (right, left) in ((slot, (turned, plain)), (slot + 2, (plain, turned))):
        rights[place] = jnp.concatenate([right[0], right[0], right[1]], axis=0)
        lefts[place] = jnp.concatenate([left[0], left[0], left[1]], axis=1)


def both_sides(waves, right, left):
    width = waves[0][0].shape[0]
    rows = jnp.concatenate([jnp.concatenate([re, im], axis=1) for re, im in waves], axis=0)
    high, low = split(rows)
    mid = jnp.dot(
        jnp.concatenate([high, low, high], axis=1), right, preferred_element_type=jnp.float32
    )
    parts = []
    for idx in range(len(waves)):
        part = mid[idx * width : (idx + 1) * width]
        parts.append(jnp.concatenate([part[:, :width], part[:, width:]], axis=0))
    cols = jnp.concatenate(parts, axis=1)
    high, low = split(cols)
    out = jnp.dot(
        left, jnp.concatenate([high, low, high], axis=0), preferred_element_type=jnp.float32
    )
    result = []
    for idx in range(len(waves)):
        part = out[:, idx * width : (idx + 1) * width]
        result.append((part[:width], part[width:]))
    return result


def wave_kernel(
    places, taps, ext, probe, measured, dft, gext, chunks,
    rights, lefts, waves, far, patch, gpatch, level, gprobe,
):
    modes, _, width, _ = probe.shape
    layers = ext.shape[0]
    records = measured.shape[0]
    count = taps.shape[1]
    reach = count // 2
    group = 4
    weight = 1.0 / (8.0 * modes)

    shape = (width, width)
    offset = lax.broadcasted_iota(jnp.int32, shape, 1) - lax.broadcasted_iota(jnp.int32, shape, 0)
    bands = [jnp.zeros(shape, jnp.float32) for _ in range(4)]
    for idx in range(count):
        ahead = offset == idx - reach
        behind = offset == reach - idx
        bands[0] = jnp.where(ahead, taps[0, idx], bands[0])
        bands[1] = jnp.where(ahead, taps[1, idx], bands[1])
        bands[2] = jnp.where(behind, taps[0, idx], bands[2])
        bands[3] = jnp.where(behind, taps[1, idx], bands[3])
    store_matrices(*bands, 0, rights, lefts)
    store_matrices(dft[0], dft[1], dft[0], dft[1], 1, rights, lefts)
    gext[...] = jnp.zeros_like(gext)
    gprobe[...] = jnp.zeros_like(gprobe)

    def one_record(rec, carry):
        row = places[rec, 0]
        col = places[rec, 1]
        block = pl.multiple_of((col // EDGE) * EDGE, EDGE)
        turn = col - block
        back = lax.rem(2 * EDGE - turn, 2 * EDGE)
        top = pl.multiple_of((row // 8) * 8, 8)
        drop = row - top
        tall = width + 8
        lift = lax.rem(tall - drop, tall)
        for layer in range(layers):
            for part in range(2):
                wide = ext[layer, part, pl.ds(top, tall), pl.ds(block, 2 * EDGE)]
                wide = pltpu.roll(wide, back, 1)[:, :width]
                patch[layer, part] = pltpu.roll(wide, lift, 0)[:width]
        gpatch[...] = jnp.zeros_like(gpatch)
        level[...] = jnp.zeros_like(level)

        def forward(step, carry):
            base = step * group
            now = [(probe[base + k, 0], probe[base + k, 1]) for k in range(group)]
            for layer in range(layers):
                obj_re, obj_im = patch[layer, 0], patch[layer, 1]
                now = [(a * obj_re - b * obj_im, a * obj_im + b * obj_re) for a, b in now]
                slot = 0 if layer + 1 < layers else 1
                now = both_sides(now, rights[slot], lefts[slot])
                for k in range(group):
                    if layer + 1 < layers:
                        waves[layer, base + k, 0] = now[k][0]
                        waves[layer, base + k, 1] = now[k][1]
                    else:
                        far[base + k, 0] = now[k][0]
                        far[base + k, 1] = now[k][1]
            total = level[...]
            for a, b in now:
                total = total + (a * a + b * b)
            level[...] = total
            return carry

        lax.fori_loop(0, modes // group, forward, 0)
        level[...] = (2.0 * weight) * (level[...] - measured[rec])

        def backward(step, carry):
            base = step * group
            scale = level[...]
            now = [(far[base + k, 0] * scale, far[base + k, 1] * scale) for k in range(group)]
            for layer in reversed(range(layers)):
                slot = 2 if layer + 1 < layers else 3
                now = both_sides(now, rights[slot], lefts[slot])
                if layer:
                    before = [
                        (waves[layer - 1, base + k, 0], waves[layer - 1, base + k, 1])
                        for k in range(group)
                    ]
                else:
                    before = [(probe[base + k, 0], probe[base + k, 1]) for k in range(group)]
                sum_re, sum_im = gpatch[layer, 0], gpatch[layer, 1]
                for (a, b), (c, d) in zip(now, before):
                    sum_re = sum_re + (a * c + b * d)
                    sum_im = sum_im + (b * c - a * d)
                gpatch[layer, 0] = sum_re
                gpatch[layer, 1] = sum_im
                obj_re, obj_im = patch[layer, 0], patch[layer, 1]
                now = [(a * obj_re + b * obj_im, b * obj_re - a * obj_im) for a, b in now]
            for k in range(group):
                gprobe[base + k, 0] += now[k][0]
                gprobe[base + k, 1] += now[k][1]
            return carry

        lax.fori_loop(0, modes // group, backward, 0)
        for layer in range(layers):
            for part in range(2):
                wide = jnp.concatenate([gpatch[layer, part], jnp.zeros((8, width), jnp.float32)], axis=0)
                wide = pltpu.roll(wide, drop, 0)
                wide = jnp.concatenate([wide, jnp.zeros((tall, width), jnp.float32)], axis=1)
                where = (layer, part, pl.ds(top, tall), pl.ds(block, 2 * EDGE))
                gext[where] = gext[where] + pltpu.roll(wide, turn, 1)
        return carry

    lax.fori_loop(0, records, one_record, 0)
    cores, chips, rows = chunks.shape[0], chunks.shape[1], chunks.shape[4]
    for chip in range(chips):
        for core in range(cores):
            first = (chip * cores + core) * rows
            chunks[core, chip] = gprobe[:, :, first : first + rows, :]


def run_records(places, taps, ext, probe, measured, chunk_shape):
    modes, _, width, _ = probe.shape
    layers = ext.shape[0]
    idx = np.arange(width)
    angle = 2.0 * math.pi / width * (idx[:, None] * idx[None, :] % width)
    dft = np.stack([np.cos(angle), -np.sin(angle)]) / math.sqrt(width)
    smem = pl.BlockSpec(memory_space=pltpu.SMEM)
    vmem = pl.BlockSpec(memory_space=pltpu.VMEM)
    f32 = jnp.float32
    return pl.pallas_call(
        wave_kernel,
        out_shape=(jax.ShapeDtypeStruct(ext.shape, f32), jax.ShapeDtypeStruct(chunk_shape, f32)),
        in_specs=[smem, smem, vmem, vmem, vmem, vmem],
        out_specs=(vmem, vmem),
        scratch_shapes=[
            pltpu.VMEM((4, 6 * width, 2 * width), jnp.bfloat16),
            pltpu.VMEM((4, 2 * width, 6 * width), jnp.bfloat16),
            pltpu.VMEM((layers - 1, modes, 2, width, width), f32),
            pltpu.VMEM((modes, 2, width, width), f32),
            pltpu.VMEM((layers, 2, width, width), f32),
            pltpu.VMEM((layers, 2, width, width), f32),
            pltpu.VMEM((width, width), f32),
            pltpu.VMEM(probe.shape, f32),
        ],
        compiler_params=pltpu.CompilerParams(vmem_limit_bytes=48 << 20),
        name="records",
    )(places, taps, ext, probe, measured, jnp.asarray(dft, f32))


def eliminate(gram_re, gram_im, probe_re, probe_im, grad_re, grad_im, scale_out):
    modes = probe_re.shape[0]
    idx = lax.broadcasted_iota(jnp.int32, (modes, modes), 0)
    lane = lax.broadcasted_iota(jnp.int32, (modes, modes), 1)
    diag = idx == lane
    w_pp, w_gg = gram_re[:modes, :modes], gram_re[modes:, modes:]
    trace_pp = jnp.sum(jnp.where(diag, w_pp, 0.0), keepdims=True)
    trace_gg = jnp.sum(jnp.where(diag, w_gg, 0.0), keepdims=True)
    factor = 0.5 * jnp.sqrt(trace_pp / (trace_gg + 1e-06))
    new_re = w_pp - factor * (gram_re[:modes, modes:] + gram_re[modes:, :modes]) + factor * factor * w_gg
    new_im = (
        gram_im[:modes, :modes]
        - factor * (gram_im[:modes, modes:] + gram_im[modes:, :modes])
        + factor * factor * gram_im[modes:, modes:]
    )
    data_re = probe_re - factor * grad_re
    data_im = factor * grad_im - probe_im
    below = lax.broadcasted_iota(jnp.int32, (modes, 1), 0)
    for step in range(modes):
        pivot = new_re[step : step + 1, step : step + 1]
        scale = 1.0 / jnp.sqrt(pivot)
        keep = below > step
        coef_re = jnp.where(keep, new_re[:, step : step + 1] * scale, 0.0)
        coef_im = jnp.where(keep, new_im[:, step : step + 1] * scale, 0.0)
        at = below == step

        def update(re, im):
            row_re = re[step : step + 1] * scale
            row_im = im[step : step + 1] * scale
            next_re = re - (coef_re * row_re - coef_im * row_im)
            next_im = im - (coef_re * row_im + coef_im * row_re)
            return jnp.where(at, row_re, next_re), jnp.where(at, row_im, next_im)

        data_re, data_im = update(data_re, data_im)
        new_re, new_im = update(new_re, new_im)
    return data_re * scale_out, data_im * (-scale_out)


def remote(src, dst, send, recv, **device):
    return pltpu.make_async_remote_copy(
        src_ref=src, dst_ref=dst, send_sem=send, recv_sem=recv,
        device_id=device, device_id_type=pl.DeviceIdType.MESH,
    )


def halo_kernel(rows, obj, ext, up_send, up_recv, down_send, down_recv, mid_send, mid_recv, top_send, top_recv, low_send, low_recv):
    layers, _, tall, wide = obj.shape
    half = EDGE // 2
    row, col = lax.axis_index("row"), lax.axis_index("col")
    mate = 1 - col
    has_up, has_down = row + 1 < rows, row > 0
    barrier = pltpu.get_barrier_semaphore()
    pl.semaphore_signal(barrier, inc=1, device_id={"col": mate}, device_id_type=pl.DeviceIdType.MESH)

    @pl.when(has_up)
    def _():
        pl.semaphore_signal(barrier, inc=1, device_id={"row": row + 1}, device_id_type=pl.DeviceIdType.MESH)

    @pl.when(has_down)
    def _():
        pl.semaphore_signal(barrier, inc=1, device_id={"row": row - 1}, device_id_type=pl.DeviceIdType.MESH)

    inner = jnp.logical_and(has_up, has_down)
    pl.when(inner)(lambda: pl.semaphore_wait(barrier, 3))
    pl.when(jnp.logical_not(inner))(lambda: pl.semaphore_wait(barrier, 2))

    own = pl.ds(EDGE, wide)
    top, mid, low = pl.ds(0, half), pl.ds(half, tall), pl.ds(half + tall, half)
    mate_src = pl.ds(pl.multiple_of(mate * (wide - EDGE), EDGE), EDGE)
    ext_src = pl.ds(pl.multiple_of(EDGE + mate * (wide - EDGE), EDGE), EDGE)
    mate_dst = pl.ds(pl.multiple_of(col * (wide + EDGE), EDGE), EDGE)
    blank = pl.ds(pl.multiple_of(col * (wide + EDGE), EDGE), EDGE)

    def up(k):
        return remote(obj.at[k, :, pl.ds(tall - half, half), :], ext.at[k, :, top, own], up_send.at[k], up_recv.at[k], row=row + 1)

    def down(k):
        return remote(obj.at[k, :, pl.ds(0, half), :], ext.at[k, :, low, own], down_send.at[k], down_recv.at[k], row=row - 1)

    def across(k):
        return remote(obj.at[k, :, :, mate_src], ext.at[k, :, mid, mate_dst], mid_send.at[k], mid_recv.at[k], col=mate)

    def across_top(k):
        return remote(ext.at[k, :, top, ext_src], ext.at[k, :, top, mate_dst], top_send.at[k], top_recv.at[k], col=mate)

    def across_low(k):
        return remote(ext.at[k, :, low, ext_src], ext.at[k, :, low, mate_dst], low_send.at[k], low_recv.at[k], col=mate)

    for k in range(layers):
        pl.when(has_up)(lambda k=k: up(k).start())
        pl.when(has_down)(lambda k=k: down(k).start())
    for k in range(layers):
        across(k).start()
    for k in range(layers):
        ext[k, :, mid, own] = obj[k]
        ext[k, :, :, blank] = jnp.zeros((2, tall + 2 * half, EDGE), jnp.float32)

    @pl.when(jnp.logical_not(has_down))
    def _():
        ext[:, :, top, :] = jnp.zeros((layers, 2, half, wide + 2 * EDGE), jnp.float32)

    @pl.when(jnp.logical_not(has_up))
    def _():
        ext[:, :, low, :] = jnp.zeros((layers, 2, half, wide + 2 * EDGE), jnp.float32)

    def pass_top(k):
        up(k).wait_recv()
        across_top(k).start()

    def pass_low(k):
        down(k).wait_recv()
        across_low(k).start()

    for k in range(layers):
        pl.when(has_down)(lambda k=k: pass_top(k))
        pl.when(has_up)(lambda k=k: pass_low(k))
    for k in range(layers):
        across(k).wait()
        pl.when(has_down)(lambda k=k: across_top(k).wait())
        pl.when(has_up)(lambda k=k: across_low(k).wait())
        pl.when(has_up)(lambda k=k: up(k).wait_send())
        pl.when(has_down)(lambda k=k: down(k).wait_send())


def run_halo(obj):
    layers, parts, tall, wide = obj.shape
    vmem = pl.BlockSpec(memory_space=pltpu.VMEM)
    return pl.pallas_call(
        functools.partial(halo_kernel, lax.axis_size("row")),
        out_shape=jax.ShapeDtypeStruct((layers, parts, tall + EDGE, wide + 2 * EDGE), jnp.float32),
        in_specs=[vmem],
        out_specs=vmem,
        scratch_shapes=[pltpu.SemaphoreType.DMA((layers,)) for _ in range(10)],
        compiler_params=pltpu.CompilerParams(
            collective_id=0, has_side_effects=True, vmem_limit_bytes=32 << 20
        ),
        name="halo",
    )(obj)


def tail_kernel(
    rows, scale_out, gext, chunks, probe, folded, out,
    from_mate, partial, parts, from_col, row_out, from_row, grams,
    half_send, half_recv, col_send, col_recv, up_send, up_recv, down_send, down_recv,
    part_send, part_recv, gram_send, gram_recv,
):
    layers, _, tall, wide = folded.shape
    half = EDGE // 2
    row, col = lax.axis_index("row"), lax.axis_index("col")
    mate = 1 - col
    has_up, has_down = row + 1 < rows, row > 0
    devices = 2 * rows
    me = row * 2 + col
    barrier = pltpu.get_barrier_semaphore()

    def greet(step, carry):
        other = lax.rem(me + step, devices)
        pl.semaphore_signal(
            barrier, inc=1, device_id={"row": other // 2, "col": lax.rem(other, 2)},
            device_id_type=pl.DeviceIdType.MESH,
        )
        return carry

    lax.fori_loop(1, devices, greet, 0)
    pl.semaphore_wait(barrier, devices - 1)

    half_copy = remote(chunks.at[mate], from_mate, half_send, half_recv, col=mate)
    half_copy.start()
    mate_part = pl.ds(pl.multiple_of(mate * (wide + EDGE), EDGE), EDGE)
    mate_part = pl.ds(pl.multiple_of((1 - col) * (wide + EDGE), EDGE), EDGE)

    def across(k):
        return remote(gext.at[k, :, :, mate_part], from_col.at[k], col_send.at[k], col_recv.at[k], col=mate)

    for k in range(layers):
        across(k).start()

    def part_copy(other, slot):
        return remote(partial.at[other], parts.at[slot], part_send.at[other], part_recv.at[slot], row=other)

    half_copy.wait()
    partial[...] = chunks[col] + from_mate[...]

    def send_part(step, carry):
        part_copy(lax.rem(row + step, rows), row).start()
        return carry

    lax.fori_loop(1, rows, send_part, 0)

    def up(k):
        return remote(row_out.at[k, 0], from_row.at[k, 0], up_send.at[k], up_recv.at[k], row=row + 1)

    def down(k):
        return remote(row_out.at[k, 1], from_row.at[k, 1], down_send.at[k], down_recv.at[k], row=row - 1)

    for k in range(layers):
        across(k).wait()
        left = gext[k, :, :, pl.ds(EDGE, EDGE)]
        right = gext[k, :, :, pl.ds(wide, EDGE)]
        arrived = from_col[k]
        left = jnp.where(col == 1, left + arrived, left)
        right = jnp.where(col == 0, right + arrived, right)
        both = jnp.concatenate([left, right], axis=2)
        folded[k] = both[:, half : half + tall]
        row_out[k, 0] = both[:, half + tall :]
        row_out[k, 1] = both[:, :half]
        pl.when(has_up)(lambda k=k: up(k).start())
        pl.when(has_down)(lambda k=k: down(k).start())

    def take_part(step, total):
        slot = lax.rem(row + step, rows)
        part_copy(slot, slot).wait_recv()
        return total + parts[slot]

    own = lax.fori_loop(1, rows, take_part, partial[row])
    pixel_rows = own.shape[2]
    parts[row] = own

    def columns(part):
        return jnp.concatenate([parts[row, :, part, r, :] for r in range(pixel_rows)], axis=1)

    grad_re, grad_im = columns(0), columns(1)
    probe_re, probe_im = probe[0], probe[1]
    stack = jnp.concatenate([probe_re, grad_re, probe_im, grad_im], axis=0)
    padded = jnp.concatenate([stack, stack, stack, stack], axis=0)
    grams[me] = lax.dot_general(
        stack, padded, (((1,), (1,)), ((), ())), precision=highest_mode, preferred_element_type=jnp.float32
    )

    def gram_copy(other, slot):
        return remote(
            grams.at[me], grams.at[slot], gram_send.at[other], gram_recv.at[slot],
            row=other // 2, col=lax.rem(other, 2),
        )

    def send_gram(step, carry):
        gram_copy(lax.rem(me + step, devices), me).start()
        return carry

    lax.fori_loop(1, devices, send_gram, 0)

    def wait_gram(step, carry):
        other = lax.rem(me + step, devices)
        gram_copy(other, other).wait_recv()
        return carry

    lax.fori_loop(1, devices, wait_gram, 0)
    total = lax.fori_loop(1, devices, lambda slot, acc: acc + grams[slot], grams[0])
    count = stack.shape[0] // 2
    gram_re = total[:count, :count] + total[count:, count : 2 * count]
    gram_im = total[:count, count : 2 * count] - total[count:, :count]
    out_re, out_im = eliminate(gram_re, gram_im, probe_re, probe_im, grad_re, grad_im, scale_out)
    out[0] = out_re
    out[1] = out_im

    def take_top(k):
        up(k).wait_recv()
        folded[k, :, :half] = folded[k, :, :half] + from_row[k, 0]

    def take_low(k):
        down(k).wait_recv()
        folded[k, :, tall - half :] = folded[k, :, tall - half :] + from_row[k, 1]

    for k in range(layers):
        pl.when(has_down)(lambda k=k: take_top(k))
        pl.when(has_up)(lambda k=k: take_low(k))
    for k in range(layers):
        pl.when(has_up)(lambda k=k: up(k).wait_send())
        pl.when(has_down)(lambda k=k: down(k).wait_send())

    def finish(step, carry):
        part_copy(lax.rem(row + step, rows), row).wait_send()
        return carry

    lax.fori_loop(1, rows, finish, 0)

    def finish_gram(step, carry):
        gram_copy(lax.rem(me + step, devices), me).wait_send()
        return carry

    lax.fori_loop(1, devices, finish_gram, 0)


def run_tail(gext, chunks, probe, tile_shape, scale_out):
    layers, parts, tall, wide = tile_shape
    _, rows, modes, _, pixel_rows, lanes = chunks.shape
    half = EDGE // 2
    f32 = jnp.float32
    vmem = pl.BlockSpec(memory_space=pltpu.VMEM)
    sems = pltpu.SemaphoreType.DMA
    return pl.pallas_call(
        functools.partial(tail_kernel, rows, scale_out),
        out_shape=(
            jax.ShapeDtypeStruct(tile_shape, f32),
            jax.ShapeDtypeStruct((2, modes, pixel_rows * lanes), f32),
        ),
        in_specs=[vmem] * 3,
        out_specs=(vmem, vmem),
        scratch_shapes=[
            pltpu.VMEM(chunks.shape[1:], f32),
            pltpu.VMEM(chunks.shape[1:], f32),
            pltpu.VMEM(chunks.shape[1:], f32),
            pltpu.VMEM((layers, parts, tall + EDGE, EDGE), f32),
            pltpu.VMEM((layers, 2, parts, half, wide), f32),
            pltpu.VMEM((layers, 2, parts, half, wide), f32),
            pltpu.VMEM((2 * rows, 4 * modes, 128), f32),
            sems, sems, sems((layers,)), sems((layers,)), sems((layers,)), sems((layers,)), sems((layers,)), sems((layers,)),
            sems((rows,)), sems((rows,)), sems((2 * rows,)), sems((2 * rows,)),
        ],
        compiler_params=pltpu.CompilerParams(
            collective_id=1, has_side_effects=True, vmem_limit_bytes=48 << 20
        ),
        name="tail",
    )(gext, chunks, probe)


def per_device(object_slices, probe, taps, measured, positions):
    modes, _, width, _ = probe.shape
    half = width // 2
    tile_rows = object_slices.shape[2]
    tile_cols = object_slices.shape[3]
    rows = lax.axis_size("row")
    ext = run_halo(object_slices)
    anchor = jnp.stack(
        [lax.axis_index("row") * tile_rows - half, lax.axis_index("col") * tile_cols - EDGE]
    )
    places = positions - anchor[None, :]
    pixel_rows = width // (2 * rows)
    chunk_shape = (2, rows, modes, 2, pixel_rows, width)
    grad_ext, chunks = run_records(places, taps, ext, probe, measured, chunk_shape)
    share = pixel_rows * width
    own_probe = lax.dynamic_slice_in_dim(probe, lax.axis_index(("row", "col")) * pixel_rows, pixel_rows, 2)
    own_probe = own_probe.reshape(modes, 2, share).transpose(1, 0, 2)
    folded, new_probe = run_tail(grad_ext, chunks, own_probe, object_slices.shape, float(width))
    return (folded, new_probe.transpose(1, 0, 2))


def solution(mesh):
    placed = (
        P(None, None, ("groups", "row"), "col"),
        P("groups", None, None, None),
        P(),
        P(("groups", "row", "col"), None, None),
        P(("groups", "row", "col"), None),
    )
    return jax.shard_map(
        per_device,
        mesh=mesh,
        in_specs=placed,
        out_specs=(P(None, None, ("groups", "row"), "col"), P("groups", None, ("row", "col"))),
        check_vma=False,
    )
```

```python
import functools
import math

import jax
import jax.numpy as jnp
import numpy as np
from jax import lax
from jax.experimental import pallas as pl
from jax.experimental.pallas import tpu as pltpu
from jax.sharding import PartitionSpec as P

highest_mode = lax.Precision.HIGHEST
EDGE = 128


def split(value):
    high = value.astype(jnp.bfloat16)
    low = (value - high.astype(jnp.float32)).astype(jnp.bfloat16)
    return high, low


def block_matrix(mat_re, mat_im):
    top = jnp.concatenate([mat_re, -mat_im], axis=1)
    bottom = jnp.concatenate([mat_im, mat_re], axis=1)
    return jnp.concatenate([top, bottom], axis=0)


def store_matrices(mat_re, mat_im, trans_re, trans_im, slot, rights, lefts):
    plain = split(block_matrix(mat_re, mat_im))
    turned = split(block_matrix(trans_re, -trans_im))
    for place, (right, left) in ((slot, (turned, plain)), (slot + 2, (plain, turned))):
        rights[place] = jnp.concatenate([right[0], right[0], right[1]], axis=0)
        lefts[place] = jnp.concatenate([left[0], left[0], left[1]], axis=1)


def both_sides(waves, right, left):
    width = waves[0][0].shape[0]
    rows = jnp.concatenate([jnp.concatenate([re, im], axis=1) for re, im in waves], axis=0)
    high, low = split(rows)
    mid = jnp.dot(
        jnp.concatenate([high, low, high], axis=1), right, preferred_element_type=jnp.float32
    )
    parts = []
    for idx in range(len(waves)):
        part = mid[idx * width : (idx + 1) * width]
        parts.append(jnp.concatenate([part[:, :width], part[:, width:]], axis=0))
    cols = jnp.concatenate(parts, axis=1)
    high, low = split(cols)
    out = jnp.dot(
        left, jnp.concatenate([high, low, high], axis=0), preferred_element_type=jnp.float32
    )
    result = []
    for idx in range(len(waves)):
        part = out[:, idx * width : (idx + 1) * width]
        result.append((part[:width], part[width:]))
    return result


def eliminate(gram_re, gram_im, probe_re, probe_im, grad_re, grad_im, scale_out):
    modes = probe_re.shape[0]
    idx = lax.broadcasted_iota(jnp.int32, (modes, modes), 0)
    lane = lax.broadcasted_iota(jnp.int32, (modes, modes), 1)
    diag = idx == lane
    w_pp, w_gg = gram_re[:modes, :modes], gram_re[modes:, modes:]
    trace_pp = jnp.sum(jnp.where(diag, w_pp, 0.0), keepdims=True)
    trace_gg = jnp.sum(jnp.where(diag, w_gg, 0.0), keepdims=True)
    factor = 0.5 * jnp.sqrt(trace_pp / (trace_gg + 1e-06))
    new_re = w_pp - factor * (gram_re[:modes, modes:] + gram_re[modes:, :modes]) + factor * factor * w_gg
    new_im = (
        gram_im[:modes, :modes]
        - factor * (gram_im[:modes, modes:] + gram_im[modes:, :modes])
        + factor * factor * gram_im[modes:, modes:]
    )
    data_re = probe_re - factor * grad_re
    data_im = factor * grad_im - probe_im
    below = lax.broadcasted_iota(jnp.int32, (modes, 1), 0)
    for step in range(modes):
        pivot = new_re[step : step + 1, step : step + 1]
        scale = 1.0 / jnp.sqrt(pivot)
        keep = below > step
        coef_re = jnp.where(keep, new_re[:, step : step + 1] * scale, 0.0)
        coef_im = jnp.where(keep, new_im[:, step : step + 1] * scale, 0.0)
        at = below == step

        def update(re, im):
            row_re = re[step : step + 1] * scale
            row_im = im[step : step + 1] * scale
            next_re = re - (coef_re * row_re - coef_im * row_im)
            next_im = im - (coef_re * row_im + coef_im * row_re)
            return jnp.where(at, row_re, next_re), jnp.where(at, row_im, next_im)

        data_re, data_im = update(data_re, data_im)
        new_re, new_im = update(new_re, new_im)
    return data_re * scale_out, data_im * (-scale_out)


def remote(src, dst, send, recv, **device):
    return pltpu.make_async_remote_copy(
        src_ref=src, dst_ref=dst, send_sem=send, recv_sem=recv,
        device_id=device, device_id_type=pl.DeviceIdType.MESH,
    )


def make_matrices(taps, dft, width, rights, lefts):
    count = taps.shape[1]
    reach = count // 2
    shape = (width, width)
    offset = lax.broadcasted_iota(jnp.int32, shape, 1) - lax.broadcasted_iota(jnp.int32, shape, 0)
    bands = [jnp.zeros(shape, jnp.float32) for _ in range(4)]
    for idx in range(count):
        ahead = offset == idx - reach
        behind = offset == reach - idx
        bands[0] = jnp.where(ahead, taps[0, idx], bands[0])
        bands[1] = jnp.where(ahead, taps[1, idx], bands[1])
        bands[2] = jnp.where(behind, taps[0, idx], bands[2])
        bands[3] = jnp.where(behind, taps[1, idx], bands[3])
    store_matrices(*bands, 0, rights, lefts)
    store_matrices(dft[0], dft[1], dft[0], dft[1], 1, rights, lefts)


def fused_kernel(
    rows, scale_out, group,
    places, taps, obj, probe, own_probe, measured, dft, folded, out,
    ext0, ext1, ext2, ext3, rights, lefts, waves, far, patch, gpatch, level, gprobe, gext,
    chunks, from_mate, partial, parts, from_col, row_out, from_row, grams,
    pick_rows, pick_cols, put_rows, put_cols,
    hup_send, hup_recv, hdown_send, hdown_recv, mid_send, mid_recv, top_send, top_recv, low_send, low_recv,
    half_send, half_recv, col_send, col_recv, up_send, up_recv, down_send, down_recv,
    part_send, part_recv, gram_send, gram_recv,
):
    exts = (ext0, ext1, ext2, ext3)
    layers, _, tall, wide = obj.shape
    modes, _, width, _ = probe.shape
    records = measured.shape[0]
    half = EDGE // 2
    row, col = lax.axis_index("row"), lax.axis_index("col")
    mate = 1 - col
    has_up, has_down = row + 1 < rows, row > 0
    devices = 2 * rows
    me = row * 2 + col
    weight = 1.0 / (8.0 * modes)
    barrier = pltpu.get_barrier_semaphore()

    def greet(step, carry):
        other = lax.rem(me + step, devices)
        pl.semaphore_signal(
            barrier, inc=1, device_id={"row": other // 2, "col": lax.rem(other, 2)},
            device_id_type=pl.DeviceIdType.MESH,
        )
        return carry

    lax.fori_loop(1, devices, greet, 0)
    pl.semaphore_wait(barrier, devices - 1)

    own = pl.ds(EDGE, wide)
    top, mid, low = pl.ds(0, half), pl.ds(half, tall), pl.ds(half + tall, half)
    mate_src = pl.ds(pl.multiple_of(mate * (wide - EDGE), EDGE), EDGE)
    ext_src = pl.ds(pl.multiple_of(EDGE + mate * (wide - EDGE), EDGE), EDGE)
    mate_dst = pl.ds(pl.multiple_of(col * (wide + EDGE), EDGE), EDGE)

    def halo_up(k):
        return remote(obj.at[k, :, pl.ds(tall - half, half), :], exts[k].at[:, top, own], hup_send.at[k], hup_recv.at[k], row=row + 1)

    def halo_down(k):
        return remote(obj.at[k, :, pl.ds(0, half), :], exts[k].at[:, low, own], hdown_send.at[k], hdown_recv.at[k], row=row - 1)

    def halo_mid(k):
        return remote(obj.at[k, :, :, mate_src], exts[k].at[:, mid, mate_dst], mid_send.at[k], mid_recv.at[k], col=mate)

    def halo_top(k):
        return remote(exts[k].at[:, top, ext_src], exts[k].at[:, top, mate_dst], top_send.at[k], top_recv.at[k], col=mate)

    def halo_low(k):
        return remote(exts[k].at[:, low, ext_src], exts[k].at[:, low, mate_dst], low_send.at[k], low_recv.at[k], col=mate)

    for k in range(layers):
        pl.when(has_up)(lambda k=k: halo_up(k).start())
        pl.when(has_down)(lambda k=k: halo_down(k).start())
        halo_mid(k).start()
    for k in range(layers):
        exts[k][:, mid, own] = obj[k]
        exts[k][:, :, mate_dst] = jnp.zeros((2, tall + 2 * half, EDGE), jnp.float32)

    @pl.when(jnp.logical_not(has_down))
    def _():
        for k in range(layers):
            exts[k][:, top, :] = jnp.zeros((2, half, wide + 2 * EDGE), jnp.float32)

    @pl.when(jnp.logical_not(has_up))
    def _():
        for k in range(layers):
            exts[k][:, low, :] = jnp.zeros((2, half, wide + 2 * EDGE), jnp.float32)

    def pass_top(k):
        halo_up(k).wait_recv()
        halo_top(k).start()

    def pass_low(k):
        halo_down(k).wait_recv()
        halo_low(k).start()

    def pass_halo(k):
        pl.when(has_down)(lambda: pass_top(k))
        pl.when(has_up)(lambda: pass_low(k))

    def end_halo(k):
        halo_mid(k).wait()
        pl.when(has_down)(lambda: halo_top(k).wait())
        pl.when(has_up)(lambda: halo_low(k).wait())
        pl.when(has_up)(lambda: halo_up(k).wait_send())
        pl.when(has_down)(lambda: halo_down(k).wait_send())

    make_matrices(taps, dft, width, rights, lefts)
    level[...] = jnp.zeros_like(level)
    pass_halo(0)

    def one_hot(shape, dim, shift):
        first = lax.broadcasted_iota(jnp.int32, shape, dim)
        second = lax.broadcasted_iota(jnp.int32, shape, 1 - dim)
        return jnp.where(first == second + shift, 1.0, 0.0).astype(jnp.bfloat16)

    full_rows, full_cols = tall + 2 * half, wide + 2 * EDGE
    for rec in range(records):
        r, c = places[rec, 0], places[rec, 1]
        pick = one_hot((width, full_rows), 1, r)
        pick_rows[rec] = jnp.concatenate([pick, pick], axis=1)
        pick = one_hot((2 * EDGE, width), 0, lax.rem(c, EDGE))
        pick_cols[rec] = jnp.concatenate([pick, pick], axis=0)
        put = one_hot((full_rows, width), 0, r)
        put_rows[rec] = jnp.concatenate([put, put], axis=1)
        put = one_hot((width, full_cols), 1, c)
        put_cols[pl.ds(rec * 2 * width, 2 * width)] = jnp.concatenate([put, put], axis=0)

    for layer in range(layers):
        end_halo(layer)
        for rec in range(records):
            start = jnp.zeros((1, 2 * EDGE), jnp.int32) + places[rec, 1]
            pieces = []
            for part in range(2):
                image = exts[layer][part]
                piece = image[:, 2 * EDGE : 4 * EDGE]
                piece = jnp.where(start < 2 * EDGE, image[:, EDGE : 3 * EDGE], piece)
                pieces.append(jnp.where(start < EDGE, image[:, : 2 * EDGE], piece))
            piece = jnp.concatenate(split(jnp.concatenate(pieces, axis=0)), axis=1)
            piece = jnp.dot(piece, pick_cols[rec], preferred_element_type=jnp.float32)
            piece = jnp.concatenate([piece[:full_rows], piece[full_rows:]], axis=1)
            piece = jnp.concatenate(split(piece), axis=0)
            piece = jnp.dot(pick_rows[rec], piece, preferred_element_type=jnp.float32)
            patch[rec, layer, 0] = piece[:, :width]
            patch[rec, layer, 1] = piece[:, width:]
        if layer + 1 < layers:
            pass_halo(layer + 1)

        def forward(step, carry, layer=layer):
            base = step * group
            now = []
            for rec in range(records):
                obj_re, obj_im = patch[rec, layer, 0], patch[rec, layer, 1]
                for k in range(group):
                    if layer:
                        a, b = waves[rec, layer - 1, base + k, 0], waves[rec, layer - 1, base + k, 1]
                    else:
                        a, b = probe[base + k, 0], probe[base + k, 1]
                    now.append((a * obj_re - b * obj_im, a * obj_im + b * obj_re))
            slot = 0 if layer + 1 < layers else 1
            now = both_sides(now, rights[slot], lefts[slot])
            for rec in range(records):
                total = None
                for k in range(group):
                    a, b = now[rec * group + k]
                    if layer + 1 < layers:
                        waves[rec, layer, base + k, 0] = a
                        waves[rec, layer, base + k, 1] = b
                    else:
                        far[rec, base + k, 0] = a
                        far[rec, base + k, 1] = b
                        power = a * a + b * b
                        total = power if total is None else total + power
                if total is not None:
                    level[rec] = level[rec] + total
            return carry

        lax.fori_loop(0, modes // group, forward, 0)

    level[...] = (2.0 * weight) * (level[...] - measured[...])
    gpatch[...] = jnp.zeros_like(gpatch)

    mate_part = pl.ds(pl.multiple_of(mate * (wide + EDGE), EDGE), EDGE)

    def across(k):
        return remote(gext.at[k, :, :, mate_part], from_col.at[k], col_send.at[k], col_recv.at[k], col=mate)

    def up(k):
        return remote(row_out.at[k, 0], from_row.at[k, 0], up_send.at[k], up_recv.at[k], row=row + 1)

    def down(k):
        return remote(row_out.at[k, 1], from_row.at[k, 1], down_send.at[k], down_recv.at[k], row=row - 1)

    def scatter(k):
        pieces = []
        for rec in range(records):
            piece = jnp.concatenate([gpatch[rec, k, 0], gpatch[rec, k, 1]], axis=1)
            piece = jnp.concatenate(split(piece), axis=0)
            piece = jnp.dot(put_rows[rec], piece, preferred_element_type=jnp.float32)
            pieces += split(jnp.concatenate([piece[:, :width], piece[:, width:]], axis=0))
        image = jnp.dot(jnp.concatenate(pieces, axis=1), put_cols[...], preferred_element_type=jnp.float32)
        gext[k, 0] = image[:full_rows]
        gext[k, 1] = image[full_rows:]

    def send_rows(k):
        across(k).wait()
        left = gext[k, :, :, pl.ds(EDGE, EDGE)]
        right = gext[k, :, :, pl.ds(wide, EDGE)]
        arrived = from_col[k]
        left = jnp.where(col == 1, left + arrived, left)
        right = jnp.where(col == 0, right + arrived, right)
        both = jnp.concatenate([left, right], axis=2)
        folded[k] = both[:, half : half + tall]
        row_out[k, 0] = both[:, half + tall :]
        row_out[k, 1] = both[:, :half]
        pl.when(has_up)(lambda: up(k).start())
        pl.when(has_down)(lambda: down(k).start())

    for layer in reversed(range(layers)):

        def backward(step, carry, layer=layer):
            base = step * group
            now = []
            for rec in range(records):
                for k in range(group):
                    a, b = far[rec, base + k, 0], far[rec, base + k, 1]
                    if layer + 1 == layers:
                        a, b = a * level[rec], b * level[rec]
                    now.append((a, b))
            slot = 2 if layer + 1 < layers else 3
            now = both_sides(now, rights[slot], lefts[slot])
            sums = [[None, None] for _ in range(group)]
            for rec in range(records):
                sum_re, sum_im = gpatch[rec, layer, 0], gpatch[rec, layer, 1]
                obj_re, obj_im = patch[rec, layer, 0], patch[rec, layer, 1]
                for k in range(group):
                    a, b = now[rec * group + k]
                    if layer:
                        c, d = waves[rec, layer - 1, base + k, 0], waves[rec, layer - 1, base + k, 1]
                    else:
                        c, d = probe[base + k, 0], probe[base + k, 1]
                    sum_re = sum_re + (a * c + b * d)
                    sum_im = sum_im + (b * c - a * d)
                    e, f = a * obj_re + b * obj_im, b * obj_re - a * obj_im
                    if layer:
                        far[rec, base + k, 0] = e
                        far[rec, base + k, 1] = f
                    elif rec:
                        sums[k] = [sums[k][0] + e, sums[k][1] + f]
                    else:
                        sums[k] = [e, f]
                gpatch[rec, layer, 0] = sum_re
                gpatch[rec, layer, 1] = sum_im
            if not layer:
                for k in range(group):
                    gprobe[base + k, 0] = sums[k][0]
                    gprobe[base + k, 1] = sums[k][1]
            return carry

        lax.fori_loop(0, modes // group, backward, 0)
        if layer:
            scatter(layer)
            across(layer).start()
            if layer + 1 < layers:
                send_rows(layer + 1)

    pixel_rows = chunks.shape[4]
    for chip in range(rows):
        for core in range(2):
            first = (chip * 2 + core) * pixel_rows
            chunks[core, chip] = gprobe[:, :, first : first + pixel_rows, :]
    half_copy = remote(chunks.at[mate], from_mate, half_send, half_recv, col=mate)
    half_copy.start()
    scatter(0)
    across(0).start()

    def part_copy(other, slot):
        return remote(partial.at[other], parts.at[slot], part_send.at[other], part_recv.at[slot], row=other)

    half_copy.wait()
    partial[...] = chunks[col] + from_mate[...]

    def send_part(step, carry):
        part_copy(lax.rem(row + step, rows), row).start()
        return carry

    lax.fori_loop(1, rows, send_part, 0)
    send_rows(1)
    send_rows(0)

    def take_part(step, total):
        slot = lax.rem(row + step, rows)
        part_copy(slot, slot).wait_recv()
        return total + parts[slot]

    parts[row] = lax.fori_loop(1, rows, take_part, partial[row])

    def columns(part):
        return jnp.concatenate([parts[row, :, part, r, :] for r in range(pixel_rows)], axis=1)

    grad_re, grad_im = columns(0), columns(1)
    probe_re, probe_im = own_probe[0], own_probe[1]
    stack = jnp.concatenate([probe_re, grad_re, probe_im, grad_im], axis=0)
    padded = jnp.concatenate([stack, stack, stack, stack], axis=0)
    grams[me] = lax.dot_general(
        stack, padded, (((1,), (1,)), ((), ())), precision=highest_mode, preferred_element_type=jnp.float32
    )

    def gram_copy(other, slot):
        return remote(
            grams.at[me], grams.at[slot], gram_send.at[other], gram_recv.at[slot],
            row=other // 2, col=lax.rem(other, 2),
        )

    def send_gram(step, carry):
        gram_copy(lax.rem(me + step, devices), me).start()
        return carry

    lax.fori_loop(1, devices, send_gram, 0)

    def take_top(k):
        up(k).wait_recv()
        folded[k, :, :half] = folded[k, :, :half] + from_row[k, 0]

    def take_low(k):
        down(k).wait_recv()
        folded[k, :, tall - half :] = folded[k, :, tall - half :] + from_row[k, 1]

    def take_rows(k):
        pl.when(has_down)(lambda: take_top(k))
        pl.when(has_up)(lambda: take_low(k))

    for k in reversed(range(1, layers)):
        take_rows(k)

    def wait_gram(step, carry):
        other = lax.rem(me + step, devices)
        gram_copy(other, other).wait_recv()
        return carry

    lax.fori_loop(1, devices, wait_gram, 0)
    total = lax.fori_loop(1, devices, lambda slot, acc: acc + grams[slot], grams[0])
    count = stack.shape[0] // 2
    gram_re = total[:count, :count] + total[count:, count : 2 * count]
    gram_im = total[:count, count : 2 * count] - total[count:, :count]
    out_re, out_im = eliminate(gram_re, gram_im, probe_re, probe_im, grad_re, grad_im, scale_out)
    out[0] = out_re
    out[1] = out_im
    take_rows(0)
    for k in range(layers):
        pl.when(has_up)(lambda k=k: up(k).wait_send())
        pl.when(has_down)(lambda k=k: down(k).wait_send())

    def finish(step, carry):
        part_copy(lax.rem(row + step, rows), row).wait_send()
        return carry

    lax.fori_loop(1, rows, finish, 0)

    def finish_gram(step, carry):
        gram_copy(lax.rem(me + step, devices), me).wait_send()
        return carry

    lax.fori_loop(1, devices, finish_gram, 0)


def per_device(object_slices, probe, taps, measured, positions):
    modes, _, width, _ = probe.shape
    half = width // 2
    layers, two, tall, wide = object_slices.shape
    records = measured.shape[0]
    rows = lax.axis_size("row")
    anchor = jnp.stack([lax.axis_index("row") * tall - half, lax.axis_index("col") * wide - EDGE])
    places = positions - anchor[None, :]
    pixel_rows = width // (2 * rows)
    share = pixel_rows * width
    own_probe = lax.dynamic_slice_in_dim(probe, lax.axis_index(("row", "col")) * pixel_rows, pixel_rows, 2)
    own_probe = own_probe.reshape(modes, 2, share).transpose(1, 0, 2)
    idx = np.arange(width)
    angle = 2.0 * math.pi / width * (idx[:, None] * idx[None, :] % width)
    dft = np.stack([np.cos(angle), -np.sin(angle)]) / math.sqrt(width)

    f32 = jnp.float32
    smem = pl.BlockSpec(memory_space=pltpu.SMEM)
    vmem = pl.BlockSpec(memory_space=pltpu.VMEM)
    sems = pltpu.SemaphoreType.DMA
    ext_shape = (two, tall + EDGE, wide + 2 * EDGE)
    chip_share = (rows, modes, 2, pixel_rows, width)
    folded, new_probe = pl.pallas_call(
        functools.partial(fused_kernel, rows, float(width), 4),
        out_shape=(
            jax.ShapeDtypeStruct(object_slices.shape, f32),
            jax.ShapeDtypeStruct((2, modes, share), f32),
        ),
        in_specs=[smem, smem] + [vmem] * 5,
        out_specs=(vmem, vmem),
        scratch_shapes=[pltpu.VMEM(ext_shape, f32) for _ in range(layers)]
        + [
            pltpu.VMEM((4, 6 * width, 2 * width), jnp.bfloat16),
            pltpu.VMEM((4, 2 * width, 6 * width), jnp.bfloat16),
            pltpu.VMEM((records, layers - 1, modes, 2, width, width), f32),
            pltpu.VMEM((records, modes, 2, width, width), f32),
            pltpu.VMEM((records, layers, 2, width, width), f32),
            pltpu.VMEM((records, layers, 2, width, width), f32),
            pltpu.VMEM((records, width, width), f32),
            pltpu.VMEM(probe.shape, f32),
            pltpu.VMEM((layers,) + ext_shape, f32),
            pltpu.VMEM((2,) + chip_share, f32),
            pltpu.VMEM(chip_share, f32),
            pltpu.VMEM(chip_share, f32),
            pltpu.VMEM(chip_share, f32),
            pltpu.VMEM((layers, two, tall + EDGE, EDGE), f32),
            pltpu.VMEM((layers, 2, two, half, wide), f32),
            pltpu.VMEM((layers, 2, two, half, wide), f32),
            pltpu.VMEM((2 * rows, 4 * modes, 128), f32),
            pltpu.VMEM((records, width, 2 * (tall + EDGE)), jnp.bfloat16),
            pltpu.VMEM((records, 4 * EDGE, width), jnp.bfloat16),
            pltpu.VMEM((records, tall + EDGE, 2 * width), jnp.bfloat16),
            pltpu.VMEM((records * 2 * width, wide + 2 * EDGE), jnp.bfloat16),
        ]
        + [sems((layers,)) for _ in range(10)]
        + [sems, sems]
        + [sems((layers,)) for _ in range(6)]
        + [sems((rows,)), sems((rows,)), sems((2 * rows,)), sems((2 * rows,))],
        compiler_params=pltpu.CompilerParams(
            collective_id=0, has_side_effects=True, vmem_limit_bytes=56 << 20
        ),
        name="fused",
    )(places, taps, object_slices, probe, own_probe, measured, jnp.asarray(dft, f32))
    return (folded, new_probe.transpose(1, 0, 2))


def solution(mesh):
    placed = (
        P(None, None, ("groups", "row"), "col"),
        P("groups", None, None, None),
        P(),
        P(("groups", "row", "col"), None, None),
        P(("groups", "row", "col"), None),
    )
    return jax.shard_map(
        per_device,
        mesh=mesh,
        in_specs=placed,
        out_specs=(P(None, None, ("groups", "row"), "col"), P("groups", None, ("row", "col"))),
        check_vma=False,
    )
```

```python
import functools
import math

import jax
import jax.numpy as jnp
import numpy as np
from jax import lax
from jax.experimental import pallas as pl
from jax.experimental.pallas import tpu as pltpu
from jax.sharding import PartitionSpec as P

highest_mode = lax.Precision.HIGHEST
EDGE = 128


def split(value):
    high = value.astype(jnp.bfloat16)
    low = (value - high.astype(jnp.float32)).astype(jnp.bfloat16)
    return high, low


def block_matrix(mat_re, mat_im):
    top = jnp.concatenate([mat_re, -mat_im], axis=1)
    bottom = jnp.concatenate([mat_im, mat_re], axis=1)
    return jnp.concatenate([top, bottom], axis=0)


def store_matrices(mat_re, mat_im, trans_re, trans_im, slot, rights, lefts):
    plain = split(block_matrix(mat_re, mat_im))
    turned = split(block_matrix(trans_re, -trans_im))
    for place, (right, left) in ((slot, (turned, plain)), (slot + 2, (plain, turned))):
        rights[place] = jnp.concatenate([right[0], right[0], right[1]], axis=0)
        lefts[place] = jnp.concatenate([left[0], left[0], left[1]], axis=1)


def both_sides(waves, right, left):
    width = waves[0][0].shape[0]
    rows = jnp.concatenate([jnp.concatenate([re, im], axis=1) for re, im in waves], axis=0)
    high, low = split(rows)
    mid = jnp.dot(
        jnp.concatenate([high, low, high], axis=1), right, preferred_element_type=jnp.float32
    )
    parts = []
    for idx in range(len(waves)):
        part = mid[idx * width : (idx + 1) * width]
        parts.append(jnp.concatenate([part[:, :width], part[:, width:]], axis=0))
    cols = jnp.concatenate(parts, axis=1)
    high, low = split(cols)
    out = jnp.dot(
        left, jnp.concatenate([high, low, high], axis=0), preferred_element_type=jnp.float32
    )
    result = []
    for idx in range(len(waves)):
        part = out[:, idx * width : (idx + 1) * width]
        result.append((part[:width], part[width:]))
    return result


def eliminate(gram_re, gram_im, probe_re, probe_im, grad_re, grad_im, scale_out):
    modes = probe_re.shape[0]
    idx = lax.broadcasted_iota(jnp.int32, (modes, modes), 0)
    lane = lax.broadcasted_iota(jnp.int32, (modes, modes), 1)
    diag = idx == lane
    w_pp, w_gg = gram_re[:modes, :modes], gram_re[modes:, modes:]
    trace_pp = jnp.sum(jnp.where(diag, w_pp, 0.0), keepdims=True)
    trace_gg = jnp.sum(jnp.where(diag, w_gg, 0.0), keepdims=True)
    factor = 0.5 * jnp.sqrt(trace_pp / (trace_gg + 1e-06))
    new_re = w_pp - factor * (gram_re[:modes, modes:] + gram_re[modes:, :modes]) + factor * factor * w_gg
    new_im = (
        gram_im[:modes, :modes]
        - factor * (gram_im[:modes, modes:] + gram_im[modes:, :modes])
        + factor * factor * gram_im[modes:, modes:]
    )
    data_re = probe_re - factor * grad_re
    data_im = factor * grad_im - probe_im
    below = lax.broadcasted_iota(jnp.int32, (modes, 1), 0)
    for step in range(modes):
        pivot = new_re[step : step + 1, step : step + 1]
        scale = 1.0 / jnp.sqrt(pivot)
        keep = below > step
        coef_re = jnp.where(keep, new_re[:, step : step + 1] * scale, 0.0)
        coef_im = jnp.where(keep, new_im[:, step : step + 1] * scale, 0.0)
        at = below == step

        def update(re, im):
            row_re = re[step : step + 1] * scale
            row_im = im[step : step + 1] * scale
            next_re = re - (coef_re * row_re - coef_im * row_im)
            next_im = im - (coef_re * row_im + coef_im * row_re)
            return jnp.where(at, row_re, next_re), jnp.where(at, row_im, next_im)

        data_re, data_im = update(data_re, data_im)
        new_re, new_im = update(new_re, new_im)
    return data_re * scale_out, data_im * (-scale_out)


def remote(src, dst, send, recv, **device):
    return pltpu.make_async_remote_copy(
        src_ref=src, dst_ref=dst, send_sem=send, recv_sem=recv,
        device_id=device, device_id_type=pl.DeviceIdType.MESH,
    )


def make_matrices(taps, dft, width, rights, lefts):
    count = taps.shape[1]
    reach = count // 2
    shape = (width, width)
    offset = lax.broadcasted_iota(jnp.int32, shape, 1) - lax.broadcasted_iota(jnp.int32, shape, 0)
    bands = [jnp.zeros(shape, jnp.float32) for _ in range(4)]
    for idx in range(count):
        ahead = offset == idx - reach
        behind = offset == reach - idx
        bands[0] = jnp.where(ahead, taps[0, idx], bands[0])
        bands[1] = jnp.where(ahead, taps[1, idx], bands[1])
        bands[2] = jnp.where(behind, taps[0, idx], bands[2])
        bands[3] = jnp.where(behind, taps[1, idx], bands[3])
    store_matrices(*bands, 0, rights, lefts)
    store_matrices(dft[0], dft[1], dft[0], dft[1], 1, rights, lefts)


def fused_kernel(
    rows, scale_out, group,
    places, taps, obj, probe, own_probe, measured, dft, folded, out,
    ext0, ext1, ext2, ext3, rights, lefts, waves, far, patch, gpatch, level, gprobe, gext,
    chunks, from_mate, partial, parts, from_col, row_out, from_row, grams,
    pick_rows, pick_cols, put_rows, put_cols,
    hup_send, hup_recv, hdown_send, hdown_recv, mid_send, mid_recv, top_send, top_recv, low_send, low_recv,
    half_send, half_recv, col_send, col_recv, up_send, up_recv, down_send, down_recv,
    part_send, part_recv, gram_send, gram_recv,
):
    exts = (ext0, ext1, ext2, ext3)
    layers, _, tall, wide = obj.shape
    modes, _, width, _ = probe.shape
    records = measured.shape[0]
    half = EDGE // 2
    row, col = lax.axis_index("row"), lax.axis_index("col")
    mate = 1 - col
    has_up, has_down = row + 1 < rows, row > 0
    devices = 2 * rows
    me = row * 2 + col
    weight = 1.0 / (8.0 * modes)
    barrier = pltpu.get_barrier_semaphore()

    def greet(step, carry):
        other = lax.rem(me + step, devices)
        pl.semaphore_signal(
            barrier, inc=1, device_id={"row": other // 2, "col": lax.rem(other, 2)},
            device_id_type=pl.DeviceIdType.MESH,
        )
        return carry

    lax.fori_loop(1, devices, greet, 0)
    pl.semaphore_wait(barrier, devices - 1)

    own = pl.ds(EDGE, wide)
    top, mid, low = pl.ds(0, half), pl.ds(half, tall), pl.ds(half + tall, half)
    mate_src = pl.ds(pl.multiple_of(mate * (wide - EDGE), EDGE), EDGE)
    ext_src = pl.ds(pl.multiple_of(EDGE + mate * (wide - EDGE), EDGE), EDGE)
    mate_dst = pl.ds(pl.multiple_of(col * (wide + EDGE), EDGE), EDGE)

    def halo_up(k):
        return remote(obj.at[k, :, pl.ds(tall - half, half), :], exts[k].at[:, top, own], hup_send.at[k], hup_recv.at[k], row=row + 1)

    def halo_down(k):
        return remote(obj.at[k, :, pl.ds(0, half), :], exts[k].at[:, low, own], hdown_send.at[k], hdown_recv.at[k], row=row - 1)

    def halo_mid(k):
        return remote(obj.at[k, :, :, mate_src], exts[k].at[:, mid, mate_dst], mid_send.at[k], mid_recv.at[k], col=mate)

    def halo_top(k):
        return remote(exts[k].at[:, top, ext_src], exts[k].at[:, top, mate_dst], top_send.at[k], top_recv.at[k], col=mate)

    def halo_low(k):
        return remote(exts[k].at[:, low, ext_src], exts[k].at[:, low, mate_dst], low_send.at[k], low_recv.at[k], col=mate)

    for k in range(layers):
        pl.when(has_up)(lambda k=k: halo_up(k).start())
        pl.when(has_down)(lambda k=k: halo_down(k).start())
        halo_mid(k).start()
    for k in range(layers):
        exts[k][:, mid, own] = obj[k]
        exts[k][:, :, mate_dst] = jnp.zeros((2, tall + 2 * half, EDGE), jnp.float32)

    @pl.when(jnp.logical_not(has_down))
    def _():
        for k in range(layers):
            exts[k][:, top, :] = jnp.zeros((2, half, wide + 2 * EDGE), jnp.float32)

    @pl.when(jnp.logical_not(has_up))
    def _():
        for k in range(layers):
            exts[k][:, low, :] = jnp.zeros((2, half, wide + 2 * EDGE), jnp.float32)

    def pass_top(k):
        halo_up(k).wait_recv()
        halo_top(k).start()

    def pass_low(k):
        halo_down(k).wait_recv()
        halo_low(k).start()

    def pass_halo(k):
        pl.when(has_down)(lambda: pass_top(k))
        pl.when(has_up)(lambda: pass_low(k))

    def end_halo(k):
        halo_mid(k).wait()
        pl.when(has_down)(lambda: halo_top(k).wait())
        pl.when(has_up)(lambda: halo_low(k).wait())
        pl.when(has_up)(lambda: halo_up(k).wait_send())
        pl.when(has_down)(lambda: halo_down(k).wait_send())

    make_matrices(taps, dft, width, rights, lefts)
    level[...] = jnp.zeros_like(level)
    pass_halo(0)

    def one_hot(shape, dim, shift):
        first = lax.broadcasted_iota(jnp.int32, shape, dim)
        second = lax.broadcasted_iota(jnp.int32, shape, 1 - dim)
        return jnp.where(first == second + shift, 1.0, 0.0).astype(jnp.bfloat16)

    full_rows, full_cols = tall + 2 * half, wide + 2 * EDGE
    for rec in range(records):
        r, c = places[rec, 0], places[rec, 1]
        pick = one_hot((width, full_rows), 1, r)
        pick_rows[rec] = jnp.concatenate([pick, pick], axis=1)
        pick = one_hot((2 * EDGE, width), 0, lax.rem(c, EDGE))
        pick_cols[rec] = jnp.concatenate([pick, pick], axis=0)
        put = one_hot((full_rows, width), 0, r)
        put_rows[rec] = jnp.concatenate([put, put], axis=1)
        put = one_hot((width, full_cols), 1, c)
        put_cols[pl.ds(rec * 2 * width, 2 * width)] = jnp.concatenate([put, put], axis=0)

    for layer in range(layers):
        end_halo(layer)
        for rec in range(records):
            start = jnp.zeros((1, 2 * EDGE), jnp.int32) + places[rec, 1]
            pieces = []
            for part in range(2):
                image = exts[layer][part]
                piece = image[:, 2 * EDGE : 4 * EDGE]
                piece = jnp.where(start < 2 * EDGE, image[:, EDGE : 3 * EDGE], piece)
                pieces.append(jnp.where(start < EDGE, image[:, : 2 * EDGE], piece))
            piece = jnp.concatenate(split(jnp.concatenate(pieces, axis=0)), axis=1)
            piece = jnp.dot(piece, pick_cols[rec], preferred_element_type=jnp.float32)
            piece = jnp.concatenate([piece[:full_rows], piece[full_rows:]], axis=1)
            piece = jnp.concatenate(split(piece), axis=0)
            piece = jnp.dot(pick_rows[rec], piece, preferred_element_type=jnp.float32)
            patch[rec, layer, 0] = piece[:, :width]
            patch[rec, layer, 1] = piece[:, width:]

        def forward(step, carry, layer=layer):
            base = step * group
            now = []
            for rec in range(records):
                obj_re, obj_im = patch[rec, layer, 0], patch[rec, layer, 1]
                for k in range(group):
                    if layer:
                        a, b = waves[rec, layer - 1, base + k, 0], waves[rec, layer - 1, base + k, 1]
                    else:
                        a, b = probe[base + k, 0], probe[base + k, 1]
                    now.append((a * obj_re - b * obj_im, a * obj_im + b * obj_re))
            slot = 0 if layer + 1 < layers else 1
            now = both_sides(now, rights[slot], lefts[slot])
            for rec in range(records):
                total = None
                for k in range(group):
                    a, b = now[rec * group + k]
                    if layer + 1 < layers:
                        waves[rec, layer, base + k, 0] = a
                        waves[rec, layer, base + k, 1] = b
                    else:
                        far[rec, base + k, 0] = a
                        far[rec, base + k, 1] = b
                        power = a * a + b * b
                        total = power if total is None else total + power
                if total is not None:
                    level[rec] = level[rec] + total
            return carry

        forward(0, 0)
        if layer + 1 < layers:
            pass_halo(layer + 1)
        lax.fori_loop(1, modes // group, forward, 0)

    level[...] = (2.0 * weight) * (level[...] - measured[...])
    gpatch[...] = jnp.zeros_like(gpatch)

    mate_part = pl.ds(pl.multiple_of(mate * (wide + EDGE), EDGE), EDGE)

    def across(k):
        return remote(gext.at[k, :, :, mate_part], from_col.at[k], col_send.at[k], col_recv.at[k], col=mate)

    def up(k):
        return remote(row_out.at[k, 0], from_row.at[k, 0], up_send.at[k], up_recv.at[k], row=row + 1)

    def down(k):
        return remote(row_out.at[k, 1], from_row.at[k, 1], down_send.at[k], down_recv.at[k], row=row - 1)

    def scatter(k):
        pieces = []
        for rec in range(records):
            piece = jnp.concatenate([gpatch[rec, k, 0], gpatch[rec, k, 1]], axis=1)
            piece = jnp.concatenate(split(piece), axis=0)
            piece = jnp.dot(put_rows[rec], piece, preferred_element_type=jnp.float32)
            pieces += split(jnp.concatenate([piece[:, :width], piece[:, width:]], axis=0))
        image = jnp.dot(jnp.concatenate(pieces, axis=1), put_cols[...], preferred_element_type=jnp.float32)
        gext[k, 0] = image[:full_rows]
        gext[k, 1] = image[full_rows:]

    def send_rows(k):
        across(k).wait()
        left = gext[k, :, :, pl.ds(EDGE, EDGE)]
        right = gext[k, :, :, pl.ds(wide, EDGE)]
        arrived = from_col[k]
        left = jnp.where(col == 1, left + arrived, left)
        right = jnp.where(col == 0, right + arrived, right)
        both = jnp.concatenate([left, right], axis=2)
        folded[k] = both[:, half : half + tall]
        row_out[k, 0] = both[:, half + tall :]
        row_out[k, 1] = both[:, :half]
        pl.when(has_up)(lambda: up(k).start())
        pl.when(has_down)(lambda: down(k).start())

    for layer in reversed(range(layers)):

        def backward(step, carry, layer=layer):
            base = step * group
            now = []
            for rec in range(records):
                for k in range(group):
                    a, b = far[rec, base + k, 0], far[rec, base + k, 1]
                    if layer + 1 == layers:
                        a, b = a * level[rec], b * level[rec]
                    now.append((a, b))
            slot = 2 if layer + 1 < layers else 3
            now = both_sides(now, rights[slot], lefts[slot])
            sums = [[None, None] for _ in range(group)]
            for rec in range(records):
                sum_re, sum_im = gpatch[rec, layer, 0], gpatch[rec, layer, 1]
                obj_re, obj_im = patch[rec, layer, 0], patch[rec, layer, 1]
                for k in range(group):
                    a, b = now[rec * group + k]
                    if layer:
                        c, d = waves[rec, layer - 1, base + k, 0], waves[rec, layer - 1, base + k, 1]
                    else:
                        c, d = probe[base + k, 0], probe[base + k, 1]
                    sum_re = sum_re + (a * c + b * d)
                    sum_im = sum_im + (b * c - a * d)
                    e, f = a * obj_re + b * obj_im, b * obj_re - a * obj_im
                    if layer:
                        far[rec, base + k, 0] = e
                        far[rec, base + k, 1] = f
                    elif rec:
                        sums[k] = [sums[k][0] + e, sums[k][1] + f]
                    else:
                        sums[k] = [e, f]
                gpatch[rec, layer, 0] = sum_re
                gpatch[rec, layer, 1] = sum_im
            if not layer:
                for k in range(group):
                    gprobe[base + k, 0] = sums[k][0]
                    gprobe[base + k, 1] = sums[k][1]
            return carry

        backward(0, 0)
        if layer + 1 < layers:
            send_rows(layer + 1)
        lax.fori_loop(1, modes // group, backward, 0)
        if layer:
            scatter(layer)
            across(layer).start()

    pixel_rows = chunks.shape[4]
    for chip in range(rows):
        for core in range(2):
            first = (chip * 2 + core) * pixel_rows
            chunks[core, chip] = gprobe[:, :, first : first + pixel_rows, :]
    half_copy = remote(chunks.at[mate], from_mate, half_send, half_recv, col=mate)
    half_copy.start()
    scatter(0)
    across(0).start()

    def part_copy(other, slot):
        return remote(partial.at[other], parts.at[slot], part_send.at[other], part_recv.at[slot], row=other)

    half_copy.wait()
    partial[...] = chunks[col] + from_mate[...]

    def send_part(step, carry):
        part_copy(lax.rem(row + step, rows), row).start()
        return carry

    lax.fori_loop(1, rows, send_part, 0)
    send_rows(0)

    def take_part(step, total):
        slot = lax.rem(row + step, rows)
        part_copy(slot, slot).wait_recv()
        return total + parts[slot]

    parts[row] = lax.fori_loop(1, rows, take_part, partial[row])

    def columns(part):
        return jnp.concatenate([parts[row, :, part, r, :] for r in range(pixel_rows)], axis=1)

    grad_re, grad_im = columns(0), columns(1)
    probe_re, probe_im = own_probe[0], own_probe[1]
    stack = jnp.concatenate([probe_re, grad_re, probe_im, grad_im], axis=0)
    padded = jnp.concatenate([stack, stack, stack, stack], axis=0)
    grams[me] = lax.dot_general(
        stack, padded, (((1,), (1,)), ((), ())), precision=highest_mode, preferred_element_type=jnp.float32
    )

    def gram_copy(other, slot):
        return remote(
            grams.at[me], grams.at[slot], gram_send.at[other], gram_recv.at[slot],
            row=other // 2, col=lax.rem(other, 2),
        )

    def send_gram(step, carry):
        gram_copy(lax.rem(me + step, devices), me).start()
        return carry

    lax.fori_loop(1, devices, send_gram, 0)

    def take_top(k):
        up(k).wait_recv()
        folded[k, :, :half] = folded[k, :, :half] + from_row[k, 0]

    def take_low(k):
        down(k).wait_recv()
        folded[k, :, tall - half :] = folded[k, :, tall - half :] + from_row[k, 1]

    def take_rows(k):
        pl.when(has_down)(lambda: take_top(k))
        pl.when(has_up)(lambda: take_low(k))

    for k in reversed(range(1, layers)):
        take_rows(k)

    def wait_gram(step, carry):
        other = lax.rem(me + step, devices)
        gram_copy(other, other).wait_recv()
        return carry

    lax.fori_loop(1, devices, wait_gram, 0)
    total = lax.fori_loop(1, devices, lambda slot, acc: acc + grams[slot], grams[0])
    count = stack.shape[0] // 2
    gram_re = total[:count, :count] + total[count:, count : 2 * count]
    gram_im = total[:count, count : 2 * count] - total[count:, :count]
    out_re, out_im = eliminate(gram_re, gram_im, probe_re, probe_im, grad_re, grad_im, scale_out)
    out[0] = out_re
    out[1] = out_im
    take_rows(0)
    for k in range(layers):
        pl.when(has_up)(lambda k=k: up(k).wait_send())
        pl.when(has_down)(lambda k=k: down(k).wait_send())

    def finish(step, carry):
        part_copy(lax.rem(row + step, rows), row).wait_send()
        return carry

    lax.fori_loop(1, rows, finish, 0)

    def finish_gram(step, carry):
        gram_copy(lax.rem(me + step, devices), me).wait_send()
        return carry

    lax.fori_loop(1, devices, finish_gram, 0)


def per_device(object_slices, probe, taps, measured, positions):
    modes, _, width, _ = probe.shape
    half = width // 2
    layers, two, tall, wide = object_slices.shape
    records = measured.shape[0]
    rows = lax.axis_size("row")
    anchor = jnp.stack([lax.axis_index("row") * tall - half, lax.axis_index("col") * wide - EDGE])
    places = positions - anchor[None, :]
    pixel_rows = width // (2 * rows)
    share = pixel_rows * width
    own_probe = lax.dynamic_slice_in_dim(probe, lax.axis_index(("row", "col")) * pixel_rows, pixel_rows, 2)
    own_probe = own_probe.reshape(modes, 2, share).transpose(1, 0, 2)
    idx = np.arange(width)
    angle = 2.0 * math.pi / width * (idx[:, None] * idx[None, :] % width)
    dft = np.stack([np.cos(angle), -np.sin(angle)]) / math.sqrt(width)

    f32 = jnp.float32
    smem = pl.BlockSpec(memory_space=pltpu.SMEM)
    vmem = pl.BlockSpec(memory_space=pltpu.VMEM)
    sems = pltpu.SemaphoreType.DMA
    ext_shape = (two, tall + EDGE, wide + 2 * EDGE)
    chip_share = (rows, modes, 2, pixel_rows, width)
    folded, new_probe = pl.pallas_call(
        functools.partial(fused_kernel, rows, float(width), 4),
        out_shape=(
            jax.ShapeDtypeStruct(object_slices.shape, f32),
            jax.ShapeDtypeStruct((2, modes, share), f32),
        ),
        in_specs=[smem, smem] + [vmem] * 5,
        out_specs=(vmem, vmem),
        scratch_shapes=[pltpu.VMEM(ext_shape, f32) for _ in range(layers)]
        + [
            pltpu.VMEM((4, 6 * width, 2 * width), jnp.bfloat16),
            pltpu.VMEM((4, 2 * width, 6 * width), jnp.bfloat16),
            pltpu.VMEM((records, layers - 1, modes, 2, width, width), f32),
            pltpu.VMEM((records, modes, 2, width, width), f32),
            pltpu.VMEM((records, layers, 2, width, width), f32),
            pltpu.VMEM((records, layers, 2, width, width), f32),
            pltpu.VMEM((records, width, width), f32),
            pltpu.VMEM(probe.shape, f32),
            pltpu.VMEM((layers,) + ext_shape, f32),
            pltpu.VMEM((2,) + chip_share, f32),
            pltpu.VMEM(chip_share, f32),
            pltpu.VMEM(chip_share, f32),
            pltpu.VMEM(chip_share, f32),
            pltpu.VMEM((layers, two, tall + EDGE, EDGE), f32),
            pltpu.VMEM((layers, 2, two, half, wide), f32),
            pltpu.VMEM((layers, 2, two, half, wide), f32),
            pltpu.VMEM((2 * rows, 4 * modes, 128), f32),
            pltpu.VMEM((records, width, 2 * (tall + EDGE)), jnp.bfloat16),
            pltpu.VMEM((records, 4 * EDGE, width), jnp.bfloat16),
            pltpu.VMEM((records, tall + EDGE, 2 * width), jnp.bfloat16),
            pltpu.VMEM((records * 2 * width, wide + 2 * EDGE), jnp.bfloat16),
        ]
        + [sems((layers,)) for _ in range(10)]
        + [sems, sems]
        + [sems((layers,)) for _ in range(6)]
        + [sems((rows,)), sems((rows,)), sems((2 * rows,)), sems((2 * rows,))],
        compiler_params=pltpu.CompilerParams(
            collective_id=0, has_side_effects=True, vmem_limit_bytes=56 << 20
        ),
        name="fused",
    )(places, taps, object_slices, probe, own_probe, measured, jnp.asarray(dft, f32))
    return (folded, new_probe.transpose(1, 0, 2))


def solution(mesh):
    placed = (
        P(None, None, ("groups", "row"), "col"),
        P("groups", None, None, None),
        P(),
        P(("groups", "row", "col"), None, None),
        P(("groups", "row", "col"), None),
    )
    return jax.shard_map(
        per_device,
        mesh=mesh,
        in_specs=placed,
        out_specs=(P(None, None, ("groups", "row"), "col"), P("groups", None, ("row", "col"))),
        check_vma=False,
    )
```
